32 devices in a mesh: dp: 4 (over y, x), ctx: 8 (over z, core).
Axes of the slice: x: 2, y: 2, z: 4, core: 2. Of those that a mesh axis runs over, the one named last changes fastest.
Arguments:
- retained_indices: int32 [4, 768], P('dp'), may hold values from 0 to 1535, as said below
- projected_result_derivative: bfloat16 [4, 1536, 2560], P('dp', 'ctx'), may hold values from -6 to 6
- head_to_model_projector: bfloat16 [4096, 2560], P('ctx'), may hold values from -0.09375 to 0.09375
- retained_queries_saved: bfloat16 [4, 768, 4096], P('dp', None, 'ctx'), may hold values from -54 to 54
- retained_keys_saved: bfloat16 [4, 768, 4096], P('dp', None, 'ctx'), may hold values from -6 to 6
- retained_values_saved: bfloat16 [4, 768, 4096], P('dp', None, 'ctx'), may hold values from -6 to 6
Outputs:
- derivative_every_place: bfloat16 [4, 1536, 12288], P('dp', 'ctx')
- projector_derivative: float32 [4096, 2560], P('ctx')
The draws below stay inside these ranges and needn't reach their ends.
Inputs may be any that keep to these rules, and one draw needn't show every extreme that they name: `retained_indices`: each row lists 768 distinct positions in increasing order. The 192 positions of one device, an aligned block, hold from 48 to 144 of them, and in every sequence some device holds exactly 144.
All inputs are finite; a program needn't handle non-finite values.
Results may differ from the reference program's by a relative error of at most 0.017.
Values may be sent and summed in bfloat16 or wider, within the bound.
A program may use at most 128 MiB of HBM per device.

```python
import math
import jax
import jax.numpy as jnp
from jax import lax

WIDTH = 2560
HEADS = 32
HEAD_DIM = 128
P_DEV = 192
FEATURES = 4096
SEQS = 4
LENGTH = 1536
SURV = 768


def draw_retained_queries_saved(key, part):
    key = jax.random.fold_in(key, 1)
    values_base = jax.random.truncated_normal(key, -6.0, 6.0, (SEQS, SURV, FEATURES), jnp.float32)
    return values_base.astype(jnp.bfloat16)


def draw_retained_keys_saved(key, part):
    key = jax.random.fold_in(key, 2)
    values_base = jax.random.truncated_normal(key, -6.0, 6.0, (SEQS, SURV, FEATURES), jnp.float32)
    return values_base.astype(jnp.bfloat16)


def draw_retained_indices(key, part):
    key = jax.random.fold_in(key, 7)
    shard_total = LENGTH // P_DEV
    lift_key, favor_key, rank_key = jax.random.split(key, 3)
    lifts = jax.random.randint(lift_key, (SEQS, shard_total), 0, P_DEV // 4 + 1)
    favored = jax.random.randint(favor_key, (SEQS, 1), 0, shard_total)
    shard_ids = jnp.arange(shard_total, dtype=jnp.int32)[None, :]
    lifts = jnp.where(shard_ids == favored, P_DEV // 4, lifts)
    lifts = jnp.where(shard_ids == (favored + 1) % shard_total, 0, lifts)
    counts = P_DEV // 2 + lifts - jnp.roll(lifts, -1, axis=1)
    local_ids = jnp.arange(LENGTH, dtype=jnp.int32) % P_DEV
    scores = jax.random.randint(rank_key, (SEQS, LENGTH), 0, 2 ** 20) * P_DEV + local_ids[None, :]
    scores = scores.reshape(SEQS, shard_total, P_DEV)
    ranks = jnp.argsort(jnp.argsort(scores, axis=-1), axis=-1)
    keep = (ranks < counts[:, :, None]).reshape(SEQS, LENGTH)
    sort_keys = jnp.where(keep, 0, LENGTH) + jnp.arange(LENGTH, dtype=jnp.int32)[None, :]
    return jnp.sort(sort_keys, axis=-1)[:, :SURV].astype(jnp.int32)


def block_levels(key, shape, cuts, least, high):
    def one(position, parts):
        heights = jax.random.uniform(jax.random.fold_in(jax.random.fold_in(key, 6), position), (parts,), jnp.float32, least / len(cuts), high / len(cuts))
        return jnp.repeat(jnp.exp(heights), shape[position] // parts).reshape((-1,) + (1,) * (len(shape) - position - 1))

    level = one(*cuts[0])
    for cut in cuts[1:]:
        level = level * one(*cut)
    return level


def bell_draw(key, dims, spread, reach, cuts=(), kind=jnp.bfloat16):
    drawn = spread * jax.random.normal(key, dims, jnp.float32)
    if cuts:
        drawn = drawn * block_levels(key, dims, cuts, -0.22, 0.18)
    return jnp.clip(drawn, -reach, reach).astype(kind)


def setup_inputs(seed: int = 0) -> dict:
    arg_keys = jax.random.split(jax.random.key(seed), 7)
    retained_indices = draw_retained_indices(jax.random.fold_in(arg_keys[6], 71), 0)
    projected_result_derivative = bell_draw(arg_keys[1], (SEQS, LENGTH, WIDTH), 1.0, 6.0, ((0, 4), (1, 8)))
    head_to_model_projector = bell_draw(arg_keys[2], (FEATURES, WIDTH), FEATURES ** -0.5, 0.09375, ((0, 8),))
    retained_queries_saved = draw_retained_queries_saved(jax.random.fold_in(arg_keys[6], 71), 0)
    retained_keys_saved = draw_retained_keys_saved(jax.random.fold_in(arg_keys[6], 71), 0)
    retained_values_saved = bell_draw(arg_keys[5], (SEQS, SURV, FEATURES), 1.0, 6.0, ((0, 4), (2, 8)))
    return dict(retained_indices=retained_indices, projected_result_derivative=projected_result_derivative, head_to_model_projector=head_to_model_projector, retained_queries_saved=retained_queries_saved, retained_keys_saved=retained_keys_saved, retained_values_saved=retained_values_saved)


def head_backward(query_head, key_head, value_head, grad_head):
    count_rows = query_head.shape[0]
    scale_factor = 1.0 / math.sqrt(HEAD_DIM)
    row_index = jnp.arange(count_rows, dtype=jnp.int32)
    allowed = row_index[None, :] <= row_index[:, None]
    scores = jnp.dot(query_head, key_head.T, preferred_element_type=jnp.float32) * scale_factor
    scores = jnp.where(allowed, scores, -jnp.inf)
    row_max = lax.optimization_barrier(jnp.max(scores, axis=-1, keepdims=True))
    exponent = jnp.exp(scores - row_max)
    probs = exponent / lax.optimization_barrier(jnp.sum(exponent, axis=-1, keepdims=True))
    probs_low = probs.astype(jnp.bfloat16)
    output = jnp.dot(probs_low, value_head, preferred_element_type=jnp.float32).astype(jnp.bfloat16)
    dprobs = jnp.dot(grad_head, value_head.T, preferred_element_type=jnp.float32)
    center = lax.optimization_barrier(jnp.sum(probs * dprobs, axis=-1, keepdims=True))
    dscores = (probs * (dprobs - center) * scale_factor).astype(jnp.bfloat16)
    grad_q = jnp.dot(dscores, key_head, preferred_element_type=jnp.float32).astype(jnp.bfloat16)
    grad_k = jnp.dot(dscores.T, query_head, preferred_element_type=jnp.float32).astype(jnp.bfloat16)
    grad_v = jnp.dot(probs_low.T, grad_head, preferred_element_type=jnp.float32).astype(jnp.bfloat16)
    return (output, grad_q, grad_k, grad_v)

def to_heads(matrix):
    return matrix.reshape(SURV, HEADS, HEAD_DIM).transpose(1, 0, 2)

def from_heads(stacked):
    return stacked.transpose(1, 0, 2).reshape(SURV, HEADS * HEAD_DIM)

def sequence_backward(sequence_places, grad_seq, query_seq, key_seq, value_seq, head_to_model_projector):
    picked = grad_seq[sequence_places]
    head_grads = jnp.dot(picked, head_to_model_projector.T, preferred_element_type=jnp.float32).astype(jnp.bfloat16)
    results = lax.map(lambda bundle: head_backward(bundle[0], bundle[1], bundle[2], bundle[3]), (to_heads(query_seq), to_heads(key_seq), to_heads(value_seq), to_heads(head_grads)))
    output, grad_q, grad_k, grad_v = [from_heads(result) for result in results]
    partial_grad = jnp.dot(output.T, picked, preferred_element_type=jnp.float32)
    joined = jnp.concatenate([grad_q, grad_k, grad_v], axis=1)
    placed = jnp.zeros((LENGTH, 3 * HEADS * HEAD_DIM), jnp.bfloat16).at[sequence_places].set(joined)
    return (placed, partial_grad)

def reference(retained_indices, projected_result_derivative, head_to_model_projector, retained_queries_saved, retained_keys_saved, retained_values_saved):

    def sequence_loop_body(running, bundle):
        placed, partial_grad = sequence_backward(bundle[0], bundle[1], bundle[2], bundle[3], bundle[4], head_to_model_projector)
        return (running + partial_grad, placed)
    initial_accumulator = jnp.zeros((HEADS * HEAD_DIM, WIDTH), jnp.float32)
    projector_derivative, derivative_every_place = lax.scan(sequence_loop_body, initial_accumulator, (retained_indices, projected_result_derivative, retained_queries_saved, retained_keys_saved, retained_values_saved))
    return (derivative_every_place, projector_derivative)
```

```python
import functools
import math

import jax
import jax.numpy as jnp
from jax import lax
from jax.experimental import pallas as pl
from jax.experimental.pallas import tpu as pltpu
from jax.sharding import PartitionSpec as P

HEAD_DIM = 128
BF = jnp.bfloat16
F32 = jnp.float32
VMEM_BYTES = 56 * 1024 * 1024


def dot_nn(a, b):
    return lax.dot_general(a, b, (((1,), (0,)), ((), ())), preferred_element_type=F32)


def dot_nt(a, b):
    return lax.dot_general(a, b, (((1,), (1,)), ((), ())), preferred_element_type=F32)


def dot_tn(a, b):
    return lax.dot_general(a, b, (((0,), (0,)), ((), ())), preferred_element_type=F32)


def query_blocks(surv):
    block = 256 if surv % 256 == 0 else surv
    return [(i * block, block) for i in range(surv // block)]


def forward_kernel(q_ref, k_ref, v_ref, probs_ref, out_ref):
    scale = 1.0 / math.sqrt(HEAD_DIM)
    for begin, size in query_blocks(q_ref.shape[0]):
        keys = begin + size
        scores = dot_nt(k_ref[0:keys, :], q_ref[begin:keys, :]) * scale
        key_at = lax.broadcasted_iota(jnp.int32, (keys, size), 0)
        query_at = lax.broadcasted_iota(jnp.int32, (keys, size), 1) + begin
        scores = jnp.where(key_at <= query_at, scores, -jnp.inf)
        exponent = jnp.exp(scores - jnp.max(scores, axis=0, keepdims=True))
        probs = exponent / jnp.sum(exponent, axis=0, keepdims=True)
        probs_ref[0, 0:keys, begin:keys] = probs
        out_ref[begin:keys, :] = dot_tn(probs.astype(BF), v_ref[0:keys, :]).astype(BF)


def forward_heads(q, k, v):
    surv, width = q.shape
    heads = width // HEAD_DIM
    rows = pl.BlockSpec((surv, HEAD_DIM), lambda h: (0, h))
    return pl.pallas_call(
        forward_kernel,
        grid=(heads,),
        in_specs=[rows] * 3,
        out_specs=[pl.BlockSpec((1, surv, surv), lambda h: (h, 0, 0)), rows],
        out_shape=[
            jax.ShapeDtypeStruct((heads, surv, surv), F32),
            jax.ShapeDtypeStruct((surv, width), BF),
        ],
        compiler_params=pltpu.CompilerParams(vmem_limit_bytes=VMEM_BYTES),
        cost_estimate=pl.CostEstimate(
            flops=heads * surv * surv * 600, bytes_accessed=heads * surv * surv * 4,
            transcendentals=heads * surv * surv
        ),
        name="forward_heads",
    )(q, k, v)


def backward_kernel(q_ref, k_ref, v_ref, g_ref, probs_ref, pack_ref, out_ref, gk, gv, joined):
    scale = 1.0 / math.sqrt(HEAD_DIM)
    surv = q_ref.shape[0]
    shards, _, room, _ = out_ref.shape
    gk[...] = jnp.zeros_like(gk)
    gv[...] = jnp.zeros_like(gv)
    for begin, size in query_blocks(surv):
        keys = begin + size
        probs = probs_ref[0, 0:keys, begin:keys]
        grads = g_ref[begin:keys, :]
        dprobs = dot_nt(v_ref[0:keys, :], grads)
        center = jnp.sum(probs * dprobs, axis=0, keepdims=True)
        dscores = (probs * (dprobs - center) * scale).astype(BF)
        joined[begin:keys, 0:HEAD_DIM] = dot_tn(dscores, k_ref[0:keys, :]).astype(BF)
        gk[0:keys, :] += dot_nn(dscores, q_ref[begin:keys, :])
        gv[0:keys, :] += dot_nn(probs.astype(BF), grads)
    joined[:, HEAD_DIM : 2 * HEAD_DIM] = gk[...].astype(BF)
    joined[:, 2 * HEAD_DIM :] = gv[...].astype(BF)
    for shard in range(shards):
        packed = dot_nn(pack_ref[shard * room : (shard + 1) * room, :], joined[...]).astype(BF)
        for part in range(3):
            out_ref[shard, part] = packed[:, part * HEAD_DIM : (part + 1) * HEAD_DIM]


def backward_heads(q, k, v, g, probs, pack, shards):
    surv, width = q.shape
    heads = width // HEAD_DIM
    room = pack.shape[0] // shards
    rows = pl.BlockSpec((surv, HEAD_DIM), lambda h: (0, h))
    return pl.pallas_call(
        backward_kernel,
        grid=(heads,),
        in_specs=[rows] * 4
        + [
            pl.BlockSpec((1, surv, surv), lambda h: (h, 0, 0)),
            pl.BlockSpec(pack.shape, lambda h: (0, 0)),
        ],
        out_specs=pl.BlockSpec((shards, 3, room, HEAD_DIM), lambda h: (0, 0, 0, h)),
        out_shape=jax.ShapeDtypeStruct((shards, 3, room, width), BF),
        scratch_shapes=[
            pltpu.VMEM((surv, HEAD_DIM), F32),
            pltpu.VMEM((surv, HEAD_DIM), F32),
            pltpu.VMEM((surv, 3 * HEAD_DIM), BF),
        ],
        compiler_params=pltpu.CompilerParams(vmem_limit_bytes=VMEM_BYTES),
        cost_estimate=pl.CostEstimate(
            flops=heads * surv * surv * 2000, bytes_accessed=heads * surv * surv * 4,
            transcendentals=0
        ),
        name="backward_heads",
    )(q, k, v, g, probs, pack)


def place_kernel(place_ref, in_ref, out_ref):
    width = in_ref.shape[3]
    for shard in range(in_ref.shape[0]):
        out_ref[:, shard * width : (shard + 1) * width] = dot_nn(
            place_ref[...], in_ref[shard, 0]
        ).astype(BF)


def place_rows(place, received):
    shards, parts, room, width = received.shape
    rows = place.shape[0]
    return pl.pallas_call(
        place_kernel,
        grid=(parts,),
        in_specs=[
            pl.BlockSpec(place.shape, lambda p: (0, 0)),
            pl.BlockSpec((shards, 1, room, width), lambda p: (0, p, 0, 0)),
        ],
        out_specs=pl.BlockSpec((rows, shards * width), lambda p: (0, p)),
        out_shape=jax.ShapeDtypeStruct((rows, parts * shards * width), BF),
        compiler_params=pltpu.CompilerParams(vmem_limit_bytes=VMEM_BYTES),
        name="place_rows",
    )(place, received)


def body(places, grads, projector, queries, keys, values):
    shards = lax.axis_size("ctx")
    me = lax.axis_index("ctx")
    places = places[0]
    surv = places.shape[0]
    rows_here = grads.shape[1]
    room = rows_here * 3 // 4

    edges = jnp.arange(shards + 1, dtype=jnp.int32) * rows_here
    first = jnp.sum((places[None, :] < edges[:, None]).astype(jnp.int32), axis=1)
    slot = jnp.arange(room, dtype=jnp.int32)
    rank = first[:-1, None] + slot[None, :]
    rank = jnp.where(rank < first[1:, None], rank, -1).reshape(-1)
    pack = (rank[:, None] == jnp.arange(surv, dtype=jnp.int32)[None, :]).astype(BF)

    mine = lax.dynamic_slice_in_dim(rank, me * room, room)
    hit = mine[:, None] == jnp.arange(surv, dtype=jnp.int32)[None, :]
    local = jnp.sum(jnp.where(hit, places[None, :] - me * rows_here + 1, 0), axis=1) - 1
    row = jnp.arange(rows_here, dtype=jnp.int32)
    place = (row[:, None] == local[None, :]).astype(BF)
    compact = (local[:, None] == row[None, :]).astype(BF)

    sent = dot_nn(compact, grads[0]).astype(BF)
    gathered = lax.all_gather(sent, "ctx", axis=0, tiled=True)

    q, k, v = queries[0], keys[0], values[0]
    probs, outputs = forward_heads(q, k, v)
    outputs = dot_nn(pack, outputs).astype(BF)

    partial = dot_tn(outputs, gathered).astype(BF)
    projector_derivative = lax.psum(partial, "dp").astype(F32)

    slot_grads = dot_nt(gathered, projector).astype(BF)
    head_grads = dot_tn(pack, slot_grads).astype(BF)
    packed = backward_heads(q, k, v, head_grads, probs, pack, shards)
    received = lax.all_to_all(packed, "ctx", split_axis=0, concat_axis=0, tiled=True)
    every_place = place_rows(place, received)
    return (every_place[None], projector_derivative)


def solution(mesh):
    in_specs = (
        P("dp", None),
        P("dp", "ctx", None),
        P("ctx", None),
        P("dp", None, "ctx"),
        P("dp", None, "ctx"),
        P("dp", None, "ctx"),
    )
    out_specs = (P("dp", "ctx", None), P("ctx", None))
    return jax.shard_map(body, mesh=mesh, in_specs=in_specs, out_specs=out_specs, check_vma=False)
```

```python
import functools
import math

import jax
import jax.numpy as jnp
from jax import lax
from jax.experimental import pallas as pl
from jax.experimental.pallas import tpu as pltpu
from jax.sharding import PartitionSpec as P

HEAD_DIM = 128
BF = jnp.bfloat16
F32 = jnp.float32
VMEM_BYTES = 56 * 1024 * 1024


def dot_nn(a, b):
    return lax.dot_general(a, b, (((1,), (0,)), ((), ())), preferred_element_type=F32)


def dot_nt(a, b):
    return lax.dot_general(a, b, (((1,), (1,)), ((), ())), preferred_element_type=F32)


def dot_tn(a, b):
    return lax.dot_general(a, b, (((0,), (0,)), ((), ())), preferred_element_type=F32)


def query_blocks(surv):
    block = 256 if surv % 256 == 0 else surv
    return [(i * block, block) for i in range(surv // block)]


def forward_kernel(q_ref, k_ref, v_ref, probs_ref, out_ref):
    scale = 1.0 / math.sqrt(HEAD_DIM)
    for begin, size in query_blocks(q_ref.shape[0]):
        keys = begin + size
        scores = dot_nt(k_ref[0:keys, :], q_ref[begin:keys, :]) * scale
        key_at = lax.broadcasted_iota(jnp.int32, (keys, size), 0)
        query_at = lax.broadcasted_iota(jnp.int32, (keys, size), 1) + begin
        scores = jnp.where(key_at <= query_at, scores, -jnp.inf)
        exponent = jnp.exp(scores - jnp.max(scores, axis=0, keepdims=True))
        probs = exponent / jnp.sum(exponent, axis=0, keepdims=True)
        probs_ref[0, 0:keys, begin:keys] = probs
        out_ref[begin:keys, :] = dot_tn(probs.astype(BF), v_ref[0:keys, :]).astype(BF)


def forward_heads(q, k, v):
    surv, width = q.shape
    heads = width // HEAD_DIM
    rows = pl.BlockSpec((surv, HEAD_DIM), lambda h: (0, h))
    return pl.pallas_call(
        forward_kernel,
        grid=(heads,),
        in_specs=[rows] * 3,
        out_specs=[pl.BlockSpec((1, surv, surv), lambda h: (h, 0, 0)), rows],
        out_shape=[
            jax.ShapeDtypeStruct((heads, surv, surv), F32),
            jax.ShapeDtypeStruct((surv, width), BF),
        ],
        compiler_params=pltpu.CompilerParams(vmem_limit_bytes=VMEM_BYTES),
        cost_estimate=pl.CostEstimate(
            flops=heads * surv * surv * 600, bytes_accessed=heads * surv * surv * 4,
            transcendentals=heads * surv * surv
        ),
        name="forward_heads",
    )(q, k, v)


def backward_kernel(
    q_ref, k_ref, v_ref, g_ref, probs_ref, pack_ref, recv_ref, gk, gv, joined, outbox, send_sem, recv_sem, own_sem
):
    head = pl.program_id(0)
    heads, shards, _, room, _ = outbox.shape
    me, group = lax.axis_index("ctx"), lax.axis_index("dp")
    peers = [lax.rem(me + offset, shards) for offset in range(1, shards)]

    @pl.when(head == 0)
    def _():
        barrier = pltpu.get_barrier_semaphore()
        for peer in peers:
            pl.semaphore_signal(
                barrier, inc=1, device_id=(group, peer), device_id_type=pl.DeviceIdType.MESH
            )
        pl.semaphore_wait(barrier, shards - 1)

    def outgoing(h, peer):
        return pltpu.make_async_remote_copy(
            src_ref=outbox.at[h, peer],
            dst_ref=recv_ref.at[me, h],
            send_sem=send_sem.at[h, peer],
            recv_sem=recv_sem.at[h, me],
            device_id=(group, peer),
            device_id_type=pl.DeviceIdType.MESH,
        )

    def incoming(h, peer):
        return pltpu.make_async_remote_copy(
            src_ref=outbox.at[h, peer],
            dst_ref=recv_ref.at[peer, h],
            send_sem=send_sem.at[h, peer],
            recv_sem=recv_sem.at[h, peer],
            device_id=(group, peer),
            device_id_type=pl.DeviceIdType.MESH,
        )

    def own(h):
        return pltpu.make_async_copy(outbox.at[h, me], recv_ref.at[me, h], own_sem.at[h])

    scale = 1.0 / math.sqrt(HEAD_DIM)
    surv = q_ref.shape[0]
    gk[...] = jnp.zeros_like(gk)
    gv[...] = jnp.zeros_like(gv)
    for begin, size in query_blocks(surv):
        keys = begin + size
        probs = probs_ref[0, 0:keys, begin:keys]
        grads = g_ref[begin:keys, :]
        dprobs = dot_nt(v_ref[0:keys, :], grads)
        center = jnp.sum(probs * dprobs, axis=0, keepdims=True)
        dscores = (probs * (dprobs - center) * scale).astype(BF)
        joined[begin:keys, 0:HEAD_DIM] = dot_tn(dscores, k_ref[0:keys, :]).astype(BF)
        gk[0:keys, :] += dot_nn(dscores, q_ref[begin:keys, :])
        gv[0:keys, :] += dot_nn(probs.astype(BF), grads)
    joined[:, HEAD_DIM : 2 * HEAD_DIM] = gk[...].astype(BF)
    joined[:, 2 * HEAD_DIM :] = gv[...].astype(BF)

    for peer in peers + [me]:
        slots = pl.ds(pl.multiple_of(peer * room, 16), room)
        packed = dot_nn(pack_ref[slots, :], joined[...]).astype(BF)
        for part in range(3):
            outbox[head, peer, part] = packed[:, part * HEAD_DIM : (part + 1) * HEAD_DIM]
        if peer is me:
            own(head).start()
        else:
            outgoing(head, peer).start()

    @pl.when(head == heads - 1)
    def _():
        for h in range(heads):
            own(h).wait()
            for peer in peers:
                outgoing(h, peer).wait_send()
                incoming(h, peer).wait_recv()


def backward_heads(q, k, v, g, probs, pack, shards):
    surv, width = q.shape
    heads = width // HEAD_DIM
    room = pack.shape[0] // shards
    rows = pl.BlockSpec((surv, HEAD_DIM), lambda h: (0, h))
    return pl.pallas_call(
        backward_kernel,
        grid=(heads,),
        in_specs=[rows] * 4
        + [
            pl.BlockSpec((1, surv, surv), lambda h: (h, 0, 0)),
            pl.BlockSpec(pack.shape, lambda h: (0, 0)),
        ],
        out_specs=pl.BlockSpec(memory_space=pl.ANY),
        out_shape=jax.ShapeDtypeStruct((shards, heads, 3, room, HEAD_DIM), BF),
        scratch_shapes=[
            pltpu.VMEM((surv, HEAD_DIM), F32),
            pltpu.VMEM((surv, HEAD_DIM), F32),
            pltpu.VMEM((surv, 3 * HEAD_DIM), BF),
            pltpu.VMEM((heads, shards, 3, room, HEAD_DIM), BF),
            pltpu.SemaphoreType.DMA((heads, shards)),
            pltpu.SemaphoreType.DMA((heads, shards)),
            pltpu.SemaphoreType.DMA((heads,)),
        ],
        compiler_params=pltpu.CompilerParams(
            vmem_limit_bytes=VMEM_BYTES, collective_id=0, has_side_effects=True
        ),
        cost_estimate=pl.CostEstimate(
            flops=heads * surv * surv * 20000, bytes_accessed=heads * surv * surv * 4,
            transcendentals=0
        ),
        name="backward_heads",
    )(q, k, v, g, probs, pack)


def place_kernel(place_ref, in_ref, out_ref):
    shards, heads, _, _, dim = in_ref.shape
    width = heads * dim
    for shard in range(shards):
        held = jnp.concatenate([in_ref[shard, h, 0] for h in range(heads)], axis=1)
        out_ref[:, shard * width : (shard + 1) * width] = dot_nn(place_ref[...], held).astype(BF)


def place_rows(place, received):
    shards, heads, parts, room, dim = received.shape
    rows = place.shape[0]
    width = shards * heads * dim
    return pl.pallas_call(
        place_kernel,
        grid=(parts,),
        in_specs=[
            pl.BlockSpec(place.shape, lambda p: (0, 0)),
            pl.BlockSpec((shards, heads, 1, room, dim), lambda p: (0, 0, p, 0, 0)),
        ],
        out_specs=pl.BlockSpec((rows, width), lambda p: (0, p)),
        out_shape=jax.ShapeDtypeStruct((rows, parts * width), BF),
        compiler_params=pltpu.CompilerParams(vmem_limit_bytes=VMEM_BYTES),
        name="place_rows",
    )(place, received)


def body(places, grads, projector, queries, keys, values):
    shards = lax.axis_size("ctx")
    me = lax.axis_index("ctx")
    places = places[0]
    surv = places.shape[0]
    rows_here = grads.shape[1]
    room = rows_here * 3 // 4

    edges = jnp.arange(shards + 1, dtype=jnp.int32) * rows_here
    first = jnp.sum((places[None, :] < edges[:, None]).astype(jnp.int32), axis=1)
    slot = jnp.arange(room, dtype=jnp.int32)
    rank = first[:-1, None] + slot[None, :]
    rank = jnp.where(rank < first[1:, None], rank, -1).reshape(-1)
    pack = (rank[:, None] == jnp.arange(surv, dtype=jnp.int32)[None, :]).astype(BF)

    mine = lax.dynamic_slice_in_dim(rank, me * room, room)
    hit = mine[:, None] == jnp.arange(surv, dtype=jnp.int32)[None, :]
    local = jnp.sum(jnp.where(hit, places[None, :] - me * rows_here + 1, 0), axis=1) - 1
    row = jnp.arange(rows_here, dtype=jnp.int32)
    place = (row[:, None] == local[None, :]).astype(BF)
    compact = (local[:, None] == row[None, :]).astype(BF)

    sent = dot_nn(compact, grads[0]).astype(BF)
    gathered = lax.all_gather(sent, "ctx", axis=0, tiled=True)

    q, k, v = queries[0], keys[0], values[0]
    probs, outputs = forward_heads(q, k, v)
    outputs = dot_nn(pack, outputs).astype(BF)

    partial = dot_tn(outputs, gathered).astype(BF)
    projector_derivative = lax.psum(partial, "dp").astype(F32)

    gathered, _ = lax.optimization_barrier((gathered, partial))
    slot_grads = dot_nt(gathered, projector).astype(BF)
    head_grads = dot_tn(pack, slot_grads).astype(BF)
    received = backward_heads(q, k, v, head_grads, probs, pack, shards)
    every_place = place_rows(place, received)
    return (every_place[None], projector_derivative)


def solution(mesh):
    in_specs = (
        P("dp", None),
        P("dp", "ctx", None),
        P("ctx", None),
        P("dp", None, "ctx"),
        P("dp", None, "ctx"),
        P("dp", None, "ctx"),
    )
    out_specs = (P("dp", "ctx", None), P("ctx", None))
    return jax.shard_map(body, mesh=mesh, in_specs=in_specs, out_specs=out_specs, check_vma=False)
```

```python
import functools
import math

import jax
import jax.numpy as jnp
from jax import lax
from jax.experimental import pallas as pl
from jax.experimental.pallas import tpu as pltpu
from jax.sharding import PartitionSpec as P

HEAD_DIM = 128
BF = jnp.bfloat16
F32 = jnp.float32
VMEM_BYTES = 56 * 1024 * 1024


def dot_nn(a, b):
    return lax.dot_general(a, b, (((1,), (0,)), ((), ())), preferred_element_type=F32)


def dot_nt(a, b):
    return lax.dot_general(a, b, (((1,), (1,)), ((), ())), preferred_element_type=F32)


def dot_tn(a, b):
    return lax.dot_general(a, b, (((0,), (0,)), ((), ())), preferred_element_type=F32)


def query_blocks(surv):
    block = 256 if surv % 256 == 0 else surv
    return [(i * block, block) for i in range(surv // block)]


def gather_kernel(
    compact_ref, grads_ref, w_ref, pack_ref, q_ref, k_ref, v_ref,
    probs_ref, head_grads_ref, partial_ref,
    blocks, stage, outputs, slot_outputs, slot_grads, total, send_sem, recv_sem, stage_sem,
):
    shards, room, _ = blocks.shape
    surv, width = q_ref.shape
    heads = width // HEAD_DIM
    me, group = lax.axis_index("ctx"), lax.axis_index("dp")
    chips = shards // 2
    chip, core = me // 2, me % 2
    other = chip * 2 + (1 - core)
    after, before = lax.rem(me + 2, shards), lax.rem(me + shards - 2, shards)

    blocks[me] = dot_nn(compact_ref[...], grads_ref[...]).astype(BF)

    barrier = pltpu.get_barrier_semaphore()
    for offset in range(1, shards):
        pl.semaphore_signal(
            barrier, inc=1, device_id=(group, lax.rem(me + offset, shards)),
            device_id_type=pl.DeviceIdType.MESH,
        )
    pl.semaphore_wait(barrier, shards - 1)

    def hop(slot, way, target):
        return pltpu.make_async_remote_copy(
            src_ref=blocks.at[slot],
            dst_ref=blocks.at[slot],
            send_sem=send_sem.at[way, slot],
            recv_sem=recv_sem.at[slot],
            device_id=(group, target),
            device_id_type=pl.DeviceIdType.MESH,
        )

    def up(slot):
        return hop(slot, 0, after)

    def down(slot):
        return hop(slot, 1, before)

    def across(slot):
        return hop(slot, 2, other)

    @pl.when(chip < chips - 1)
    def _():
        up(me).start()

    @pl.when(chip > 0)
    def _():
        down(me).start()

    across(me).start()

    scale = 1.0 / math.sqrt(HEAD_DIM)

    def keep(head):
        return pltpu.make_async_copy(stage, probs_ref.at[head], stage_sem)

    def forward(head, carry):
        lanes = pl.ds(pl.multiple_of(head * HEAD_DIM, HEAD_DIM), HEAD_DIM)

        @pl.when(head > 0)
        def _():
            keep(head - 1).wait()

        for begin, size in query_blocks(surv):
            keys = begin + size
            scores = dot_nt(k_ref[0:keys, lanes], q_ref[begin:keys, lanes]) * scale
            key_at = lax.broadcasted_iota(jnp.int32, (keys, size), 0)
            query_at = lax.broadcasted_iota(jnp.int32, (keys, size), 1) + begin
            scores = jnp.where(key_at <= query_at, scores, -jnp.inf)
            exponent = jnp.exp(scores - jnp.max(scores, axis=0, keepdims=True))
            probs = exponent / jnp.sum(exponent, axis=0, keepdims=True)
            stage[0:keys, begin:keys] = probs
            outputs[begin:keys, lanes] = dot_tn(probs.astype(BF), v_ref[0:keys, lanes]).astype(BF)
        keep(head).start()
        return carry

    lax.fori_loop(0, heads, forward, 0)
    slot_outputs[...] = dot_nn(pack_ref[...], outputs[...]).astype(BF)
    keep(heads - 1).wait()

    def work(slot):
        rows = pl.ds(pl.multiple_of(slot * room, 16), room)
        slot_grads[rows, :] = dot_nt(blocks[slot], w_ref[...]).astype(BF)
        total[...] += dot_tn(slot_outputs[rows, :], blocks[slot])

    total[...] = jnp.zeros_like(total)
    work(me)
    across(other).wait_recv()
    work(other)

    def step(distance, carry):
        lower, upper = chip - distance, chip + distance

        @pl.when(lower >= 0)
        def _():
            slot = lower * 2 + core
            up(slot).wait_recv()

            @pl.when(chip < chips - 1)
            def _():
                up(slot).start()

            across(slot).start()

        @pl.when(upper < chips)
        def _():
            slot = upper * 2 + core
            down(slot).wait_recv()

            @pl.when(chip > 0)
            def _():
                down(slot).start()

            across(slot).start()

        def each(which, inner):
            source = chip + (2 * (which % 2) - 1) * distance
            from_other = which // 2
            slot = source * 2 + core + from_other * (1 - 2 * core)

            @pl.when((source >= 0) & (source < chips))
            def _():
                @pl.when(from_other == 1)
                def _():
                    across(slot).wait_recv()

                work(slot)

            return inner

        lax.fori_loop(0, 4, each, 0)
        return carry

    lax.fori_loop(1, chips, step, 0)

    head_grads_ref[...] = dot_tn(pack_ref[...], slot_grads[...]).astype(BF)
    partial_ref[...] = total[...].astype(BF)

    across(me).wait_send()

    @pl.when(chip < chips - 1)
    def _():
        up(me).wait_send()

    @pl.when(chip > 0)
    def _():
        down(me).wait_send()

    def finish(distance, carry):
        lower, upper = chip - distance, chip + distance

        @pl.when(lower >= 0)
        def _():
            across(lower * 2 + core).wait_send()

            @pl.when(chip < chips - 1)
            def _():
                up(lower * 2 + core).wait_send()

        @pl.when(upper < chips)
        def _():
            across(upper * 2 + core).wait_send()

            @pl.when(chip > 0)
            def _():
                down(upper * 2 + core).wait_send()

        return carry

    lax.fori_loop(1, chips, finish, 0)


def gather_forward(compact, grads, w, pack, q, k, v, shards):
    surv, width = q.shape
    heads = width // HEAD_DIM
    room = compact.shape[0]
    model = grads.shape[1]
    whole = pl.BlockSpec(memory_space=pltpu.VMEM)
    return pl.pallas_call(
        gather_kernel,
        in_specs=[whole] * 7,
        out_specs=[pl.BlockSpec(memory_space=pl.ANY), whole, whole],
        out_shape=[
            jax.ShapeDtypeStruct((heads, surv, surv), F32),
            jax.ShapeDtypeStruct((surv, width), BF),
            jax.ShapeDtypeStruct((width, model), BF),
        ],
        scratch_shapes=[
            pltpu.VMEM((shards, room, model), BF),
            pltpu.VMEM((surv, surv), F32),
            pltpu.VMEM((surv, width), BF),
            pltpu.VMEM((shards * room, width), BF),
            pltpu.VMEM((shards * room, width), BF),
            pltpu.VMEM((width, model), F32),
            pltpu.SemaphoreType.DMA((3, shards)),
            pltpu.SemaphoreType.DMA((shards,)),
            pltpu.SemaphoreType.DMA,
        ],
        compiler_params=pltpu.CompilerParams(
            vmem_limit_bytes=VMEM_BYTES, collective_id=1, has_side_effects=True
        ),
        name="gather_forward",
    )(compact, grads, w, pack, q, k, v)


def backward_kernel(
    q_ref, k_ref, v_ref, g_ref, probs_ref, pack_ref, recv_ref, gk, gv, joined, outbox, send_sem, recv_sem, own_sem
):
    head = pl.program_id(0)
    heads, shards, _, room, _ = outbox.shape
    me, group = lax.axis_index("ctx"), lax.axis_index("dp")
    peers = [lax.rem(me + offset, shards) for offset in range(1, shards)]

    @pl.when(head == 0)
    def _():
        barrier = pltpu.get_barrier_semaphore()
        for peer in peers:
            pl.semaphore_signal(
                barrier, inc=1, device_id=(group, peer), device_id_type=pl.DeviceIdType.MESH
            )
        pl.semaphore_wait(barrier, shards - 1)

    def outgoing(h, peer):
        return pltpu.make_async_remote_copy(
            src_ref=outbox.at[h, peer],
            dst_ref=recv_ref.at[me, h],
            send_sem=send_sem.at[h, peer],
            recv_sem=recv_sem.at[h, me],
            device_id=(group, peer),
            device_id_type=pl.DeviceIdType.MESH,
        )

    def incoming(h, peer):
        return pltpu.make_async_remote_copy(
            src_ref=outbox.at[h, peer],
            dst_ref=recv_ref.at[peer, h],
            send_sem=send_sem.at[h, peer],
            recv_sem=recv_sem.at[h, peer],
            device_id=(group, peer),
            device_id_type=pl.DeviceIdType.MESH,
        )

    def own(h):
        return pltpu.make_async_copy(outbox.at[h, me], recv_ref.at[me, h], own_sem.at[h])

    scale = 1.0 / math.sqrt(HEAD_DIM)
    surv = q_ref.shape[0]
    gk[...] = jnp.zeros_like(gk)
    gv[...] = jnp.zeros_like(gv)
    for begin, size in query_blocks(surv):
        keys = begin + size
        probs = probs_ref[0, 0:keys, begin:keys]
        grads = g_ref[begin:keys, :]
        dprobs = dot_nt(v_ref[0:keys, :], grads)
        center = jnp.sum(probs * dprobs, axis=0, keepdims=True)
        dscores = (probs * (dprobs - center) * scale).astype(BF)
        joined[begin:keys, 0:HEAD_DIM] = dot_tn(dscores, k_ref[0:keys, :]).astype(BF)
        gk[0:keys, :] += dot_nn(dscores, q_ref[begin:keys, :])
        gv[0:keys, :] += dot_nn(probs.astype(BF), grads)
    joined[:, HEAD_DIM : 2 * HEAD_DIM] = gk[...].astype(BF)
    joined[:, 2 * HEAD_DIM :] = gv[...].astype(BF)

    for peer in peers + [me]:
        slots = pl.ds(pl.multiple_of(peer * room, 16), room)
        packed = dot_nn(pack_ref[slots, :], joined[...]).astype(BF)
        for part in range(3):
            outbox[head, peer, part] = packed[:, part * HEAD_DIM : (part + 1) * HEAD_DIM]
        if peer is me:
            own(head).start()
        else:
            outgoing(head, peer).start()

    @pl.when(head == heads - 1)
    def _():
        for h in range(heads):
            own(h).wait()
            for peer in peers:
                outgoing(h, peer).wait_send()
                incoming(h, peer).wait_recv()


def backward_heads(q, k, v, g, probs, pack, shards):
    surv, width = q.shape
    heads = width // HEAD_DIM
    room = pack.shape[0] // shards
    rows = pl.BlockSpec((surv, HEAD_DIM), lambda h: (0, h))
    return pl.pallas_call(
        backward_kernel,
        grid=(heads,),
        in_specs=[rows] * 4
        + [
            pl.BlockSpec((1, surv, surv), lambda h: (h, 0, 0)),
            pl.BlockSpec(pack.shape, lambda h: (0, 0)),
        ],
        out_specs=pl.BlockSpec(memory_space=pl.ANY),
        out_shape=jax.ShapeDtypeStruct((shards, heads, 3, room, HEAD_DIM), BF),
        scratch_shapes=[
            pltpu.VMEM((surv, HEAD_DIM), F32),
            pltpu.VMEM((surv, HEAD_DIM), F32),
            pltpu.VMEM((surv, 3 * HEAD_DIM), BF),
            pltpu.VMEM((heads, shards, 3, room, HEAD_DIM), BF),
            pltpu.SemaphoreType.DMA((heads, shards)),
            pltpu.SemaphoreType.DMA((heads, shards)),
            pltpu.SemaphoreType.DMA((heads,)),
        ],
        compiler_params=pltpu.CompilerParams(
            vmem_limit_bytes=VMEM_BYTES, collective_id=0, has_side_effects=True
        ),
        cost_estimate=pl.CostEstimate(
            flops=heads * surv * surv * 20000, bytes_accessed=heads * surv * surv * 4,
            transcendentals=0
        ),
        name="backward_heads",
    )(q, k, v, g, probs, pack)


def place_kernel(place_ref, in_ref, out_ref):
    shards, heads, _, _, dim = in_ref.shape
    width = heads * dim
    for shard in range(shards):
        held = jnp.concatenate([in_ref[shard, h, 0] for h in range(heads)], axis=1)
        out_ref[:, shard * width : (shard + 1) * width] = dot_nn(place_ref[...], held).astype(BF)


def place_rows(place, received):
    shards, heads, parts, room, dim = received.shape
    rows = place.shape[0]
    width = shards * heads * dim
    return pl.pallas_call(
        place_kernel,
        grid=(parts,),
        in_specs=[
            pl.BlockSpec(place.shape, lambda p: (0, 0)),
            pl.BlockSpec((shards, heads, 1, room, dim), lambda p: (0, 0, p, 0, 0)),
        ],
        out_specs=pl.BlockSpec((rows, width), lambda p: (0, p)),
        out_shape=jax.ShapeDtypeStruct((rows, parts * width), BF),
        compiler_params=pltpu.CompilerParams(vmem_limit_bytes=VMEM_BYTES),
        name="place_rows",
    )(place, received)


def body(places, grads, projector, queries, keys, values):
    shards = lax.axis_size("ctx")
    me = lax.axis_index("ctx")
    places = places[0]
    surv = places.shape[0]
    rows_here = grads.shape[1]
    room = rows_here * 3 // 4

    edges = jnp.arange(shards + 1, dtype=jnp.int32) * rows_here
    first = jnp.sum((places[None, :] < edges[:, None]).astype(jnp.int32), axis=1)
    slot = jnp.arange(room, dtype=jnp.int32)
    rank = first[:-1, None] + slot[None, :]
    rank = jnp.where(rank < first[1:, None], rank, -1).reshape(-1)
    pack = (rank[:, None] == jnp.arange(surv, dtype=jnp.int32)[None, :]).astype(BF)

    mine = lax.dynamic_slice_in_dim(rank, me * room, room)
    hit = mine[:, None] == jnp.arange(surv, dtype=jnp.int32)[None, :]
    local = jnp.sum(jnp.where(hit, places[None, :] - me * rows_here + 1, 0), axis=1) - 1
    row = jnp.arange(rows_here, dtype=jnp.int32)
    place = (row[:, None] == local[None, :]).astype(BF)
    compact = (local[:, None] == row[None, :]).astype(BF)

    q, k, v = queries[0], keys[0], values[0]
    probs, head_grads, partial = gather_forward(
        compact, grads[0], projector, pack, q, k, v, shards
    )
    projector_derivative = lax.psum(partial, "dp").astype(F32)
    received = backward_heads(q, k, v, head_grads, probs, pack, shards)
    every_place = place_rows(place, received)
    return (every_place[None], projector_derivative)


def solution(mesh):
    in_specs = (
        P("dp", None),
        P("dp", "ctx", None),
        P("ctx", None),
        P("dp", None, "ctx"),
        P("dp", None, "ctx"),
        P("dp", None, "ctx"),
    )
    out_specs = (P("dp", "ctx", None), P("ctx", None))
    return jax.shard_map(body, mesh=mesh, in_specs=in_specs, out_specs=out_specs, check_vma=False)
```

```python
import functools
import math

import jax
import jax.numpy as jnp
from jax import lax
from jax.experimental import pallas as pl
from jax.experimental.pallas import tpu as pltpu
from jax.sharding import PartitionSpec as P

HEAD_DIM = 128
BF = jnp.bfloat16
F32 = jnp.float32
VMEM_BYTES = 56 * 1024 * 1024


def dot_nn(a, b):
    return lax.dot_general(a, b, (((1,), (0,)), ((), ())), preferred_element_type=F32)


def dot_nt(a, b):
    return lax.dot_general(a, b, (((1,), (1,)), ((), ())), preferred_element_type=F32)


def dot_tn(a, b):
    return lax.dot_general(a, b, (((0,), (0,)), ((), ())), preferred_element_type=F32)


def query_blocks(surv):
    block = 256 if surv % 256 == 0 else surv
    return [(i * block, block) for i in range(surv // block)]


def gather_kernel(
    compact_ref, grads_ref, w_ref, pack_ref, q_ref, k_ref, v_ref,
    probs_ref, head_grads_ref, partial_ref,
    blocks, stage, outputs, slot_outputs, slot_grads, total, send_sem, recv_sem, stage_sem,
):
    shards, room, _ = blocks.shape
    surv, width = q_ref.shape
    heads = width // HEAD_DIM
    me, group = lax.axis_index("ctx"), lax.axis_index("dp")
    chips = shards // 2
    chip, core = me // 2, me % 2
    other = chip * 2 + (1 - core)
    after, before = lax.rem(me + 2, shards), lax.rem(me + shards - 2, shards)

    blocks[me] = dot_nn(compact_ref[...], grads_ref[...]).astype(BF)

    barrier = pltpu.get_barrier_semaphore()
    for offset in range(1, shards):
        pl.semaphore_signal(
            barrier, inc=1, device_id=(group, lax.rem(me + offset, shards)),
            device_id_type=pl.DeviceIdType.MESH,
        )
    pl.semaphore_wait(barrier, shards - 1)

    def hop(slot, way, target):
        return pltpu.make_async_remote_copy(
            src_ref=blocks.at[slot],
            dst_ref=blocks.at[slot],
            send_sem=send_sem.at[way, slot],
            recv_sem=recv_sem.at[slot],
            device_id=(group, target),
            device_id_type=pl.DeviceIdType.MESH,
        )

    def up(slot):
        return hop(slot, 0, after)

    def down(slot):
        return hop(slot, 1, before)

    def across(slot):
        return hop(slot, 2, other)

    @pl.when(chip < chips - 1)
    def _():
        up(me).start()

    @pl.when(chip > 0)
    def _():
        down(me).start()

    across(me).start()

    scale = 1.0 / math.sqrt(HEAD_DIM)

    def keep(head):
        return pltpu.make_async_copy(stage, probs_ref.at[head], stage_sem)

    def forward(head, carry):
        lanes = pl.ds(pl.multiple_of(head * HEAD_DIM, HEAD_DIM), HEAD_DIM)

        @pl.when(head > 0)
        def _():
            keep(head - 1).wait()

        for begin, size in query_blocks(surv):
            keys = begin + size
            scores = dot_nt(k_ref[0:keys, lanes], q_ref[begin:keys, lanes]) * scale
            key_at = lax.broadcasted_iota(jnp.int32, (keys, size), 0)
            query_at = lax.broadcasted_iota(jnp.int32, (keys, size), 1) + begin
            scores = jnp.where(key_at <= query_at, scores, -jnp.inf)
            exponent = jnp.exp(scores - jnp.max(scores, axis=0, keepdims=True))
            probs = exponent / jnp.sum(exponent, axis=0, keepdims=True)
            stage[0:keys, begin:keys] = probs
            outputs[begin:keys, lanes] = dot_tn(probs.astype(BF), v_ref[0:keys, lanes]).astype(BF)
        keep(head).start()
        return carry

    lax.fori_loop(0, heads, forward, 0)
    slot_outputs[...] = dot_nn(pack_ref[...], outputs[...]).astype(BF)
    keep(heads - 1).wait()

    def work(slot):
        rows = pl.ds(pl.multiple_of(slot * room, 16), room)
        slot_grads[rows, :] = dot_nt(blocks[slot], w_ref[...]).astype(BF)
        total[...] += dot_tn(slot_outputs[rows, :], blocks[slot])

    total[...] = jnp.zeros_like(total)
    work(me)
    across(other).wait_recv()
    work(other)

    def step(distance, carry):
        lower, upper = chip - distance, chip + distance

        @pl.when(lower >= 0)
        def _():
            slot = lower * 2 + core
            up(slot).wait_recv()

            @pl.when(chip < chips - 1)
            def _():
                up(slot).start()

            across(slot).start()

        @pl.when(upper < chips)
        def _():
            slot = upper * 2 + core
            down(slot).wait_recv()

            @pl.when(chip > 0)
            def _():
                down(slot).start()

            across(slot).start()

        def each(which, inner):
            source = chip + (2 * (which % 2) - 1) * distance
            from_other = which // 2
            slot = source * 2 + core + from_other * (1 - 2 * core)

            @pl.when((source >= 0) & (source < chips))
            def _():
                @pl.when(from_other == 1)
                def _():
                    across(slot).wait_recv()

                work(slot)

            return inner

        lax.fori_loop(0, 4, each, 0)
        return carry

    lax.fori_loop(1, chips, step, 0)

    head_grads_ref[...] = dot_tn(pack_ref[...], slot_grads[...]).astype(BF)
    partial_ref[...] = total[...].astype(BF)

    across(me).wait_send()

    @pl.when(chip < chips - 1)
    def _():
        up(me).wait_send()

    @pl.when(chip > 0)
    def _():
        down(me).wait_send()

    def finish(distance, carry):
        lower, upper = chip - distance, chip + distance

        @pl.when(lower >= 0)
        def _():
            across(lower * 2 + core).wait_send()

            @pl.when(chip < chips - 1)
            def _():
                up(lower * 2 + core).wait_send()

        @pl.when(upper < chips)
        def _():
            across(upper * 2 + core).wait_send()

            @pl.when(chip > 0)
            def _():
                down(upper * 2 + core).wait_send()

        return carry

    lax.fori_loop(1, chips, finish, 0)


def gather_forward(compact, grads, w, pack, q, k, v, shards):
    surv, width = q.shape
    heads = width // HEAD_DIM
    room = compact.shape[0]
    model = grads.shape[1]
    whole = pl.BlockSpec(memory_space=pltpu.VMEM)
    return pl.pallas_call(
        gather_kernel,
        in_specs=[whole] * 7,
        out_specs=[pl.BlockSpec(memory_space=pl.ANY), whole, whole],
        out_shape=[
            jax.ShapeDtypeStruct((heads, surv, surv), F32),
            jax.ShapeDtypeStruct((surv, width), BF),
            jax.ShapeDtypeStruct((width, model), BF),
        ],
        scratch_shapes=[
            pltpu.VMEM((shards, room, model), BF),
            pltpu.VMEM((surv, surv), F32),
            pltpu.VMEM((surv, width), BF),
            pltpu.VMEM((shards * room, width), BF),
            pltpu.VMEM((shards * room, width), BF),
            pltpu.VMEM((width, model), F32),
            pltpu.SemaphoreType.DMA((3, shards)),
            pltpu.SemaphoreType.DMA((shards,)),
            pltpu.SemaphoreType.DMA,
        ],
        compiler_params=pltpu.CompilerParams(
            vmem_limit_bytes=VMEM_BYTES, collective_id=1, has_side_effects=True
        ),
        name="gather_forward",
    )(compact, grads, w, pack, q, k, v)


def backward_kernel(
    q_ref, k_ref, v_ref, g_ref, probs_ref, pack_ref, partial_ref,
    recv_ref, sum_ref,
    gk, gv, joined, outbox, inbox, summed,
    send_sem, recv_sem, own_sem, sum_send, sum_recv, sum_own,
):
    head = pl.program_id(0)
    heads, shards, _, room, _ = outbox.shape
    me, group = lax.axis_index("ctx"), lax.axis_index("dp")
    peers = [lax.rem(me + offset, shards) for offset in range(1, shards)]
    groups, piece, _ = inbox.shape
    others = [lax.rem(group + offset, groups) for offset in range(1, groups)]

    def piece_rows(owner):
        return pl.ds(pl.multiple_of(owner * piece, 16), piece)

    def scatter(owner, source):
        return pltpu.make_async_remote_copy(
            src_ref=partial_ref.at[piece_rows(owner)],
            dst_ref=inbox.at[source],
            send_sem=sum_send.at[0, owner],
            recv_sem=sum_recv.at[0, source],
            device_id=(owner, me),
            device_id_type=pl.DeviceIdType.MESH,
        )

    def spread(target, owner):
        return pltpu.make_async_remote_copy(
            src_ref=summed,
            dst_ref=sum_ref.at[piece_rows(owner)],
            send_sem=sum_send.at[1, target],
            recv_sem=sum_recv.at[1, owner],
            device_id=(target, me),
            device_id_type=pl.DeviceIdType.MESH,
        )

    scatter_own = pltpu.make_async_copy(
        partial_ref.at[piece_rows(group)], inbox.at[group], sum_own.at[0]
    )
    spread_own = pltpu.make_async_copy(summed, sum_ref.at[piece_rows(group)], sum_own.at[1])

    @pl.when(head == 0)
    def _():
        barrier = pltpu.get_barrier_semaphore()
        for peer in peers:
            pl.semaphore_signal(
                barrier, inc=1, device_id=(group, peer), device_id_type=pl.DeviceIdType.MESH
            )
        for target in others:
            pl.semaphore_signal(
                barrier, inc=1, device_id=(target, me), device_id_type=pl.DeviceIdType.MESH
            )
        pl.semaphore_wait(barrier, shards - 1 + groups - 1)
        for owner in others:
            scatter(owner, group).start()
        scatter_own.start()

    def outgoing(h, peer):
        return pltpu.make_async_remote_copy(
            src_ref=outbox.at[h, peer],
            dst_ref=recv_ref.at[me, h],
            send_sem=send_sem.at[h, peer],
            recv_sem=recv_sem.at[h, me],
            device_id=(group, peer),
            device_id_type=pl.DeviceIdType.MESH,
        )

    def incoming(h, peer):
        return pltpu.make_async_remote_copy(
            src_ref=outbox.at[h, peer],
            dst_ref=recv_ref.at[peer, h],
            send_sem=send_sem.at[h, peer],
            recv_sem=recv_sem.at[h, peer],
            device_id=(group, peer),
            device_id_type=pl.DeviceIdType.MESH,
        )

    def own(h):
        return pltpu.make_async_copy(outbox.at[h, me], recv_ref.at[me, h], own_sem.at[h])

    scale = 1.0 / math.sqrt(HEAD_DIM)
    surv = q_ref.shape[0]
    gk[...] = jnp.zeros_like(gk)
    gv[...] = jnp.zeros_like(gv)
    for begin, size in query_blocks(surv):
        keys = begin + size
        probs = probs_ref[0, 0:keys, begin:keys]
        grads = g_ref[begin:keys, :]
        dprobs = dot_nt(v_ref[0:keys, :], grads)
        center = jnp.sum(probs * dprobs, axis=0, keepdims=True)
        dscores = (probs * (dprobs - center) * scale).astype(BF)
        joined[begin:keys, 0:HEAD_DIM] = dot_tn(dscores, k_ref[0:keys, :]).astype(BF)
        gk[0:keys, :] += dot_nn(dscores, q_ref[begin:keys, :])
        gv[0:keys, :] += dot_nn(probs.astype(BF), grads)
    joined[:, HEAD_DIM : 2 * HEAD_DIM] = gk[...].astype(BF)
    joined[:, 2 * HEAD_DIM :] = gv[...].astype(BF)

    for peer in peers + [me]:
        slots = pl.ds(pl.multiple_of(peer * room, 16), room)
        packed = dot_nn(pack_ref[slots, :], joined[...]).astype(BF)
        for part in range(3):
            outbox[head, peer, part] = packed[:, part * HEAD_DIM : (part + 1) * HEAD_DIM]
        if peer is me:
            own(head).start()
        else:
            outgoing(head, peer).start()

    @pl.when(head == heads - 1)
    def _():
        scatter_own.wait()
        for source in others:
            scatter(source, source).wait_recv()
        run = inbox[0].astype(F32)
        for source in range(1, groups):
            run = run + inbox[source].astype(F32)
        summed[...] = run.astype(BF)
        for target in others:
            spread(target, group).start()
        spread_own.start()
        for h in range(heads):
            own(h).wait()
            for peer in peers:
                outgoing(h, peer).wait_send()
                incoming(h, peer).wait_recv()
        for target in others:
            scatter(target, group).wait_send()
            spread(target, group).wait_send()
            spread(target, target).wait_recv()
        spread_own.wait()


def backward_heads(q, k, v, g, probs, pack, partial, shards, groups):
    surv, width = q.shape
    heads = width // HEAD_DIM
    room = pack.shape[0] // shards
    rows = pl.BlockSpec((surv, HEAD_DIM), lambda h: (0, h))
    return pl.pallas_call(
        backward_kernel,
        grid=(heads,),
        in_specs=[rows] * 4
        + [
            pl.BlockSpec((1, surv, surv), lambda h: (h, 0, 0)),
            pl.BlockSpec(pack.shape, lambda h: (0, 0)),
            pl.BlockSpec(memory_space=pl.ANY),
        ],
        out_specs=[pl.BlockSpec(memory_space=pl.ANY)] * 2,
        out_shape=[
            jax.ShapeDtypeStruct((shards, heads, 3, room, HEAD_DIM), BF),
            jax.ShapeDtypeStruct(partial.shape, BF),
        ],
        scratch_shapes=[
            pltpu.VMEM((surv, HEAD_DIM), F32),
            pltpu.VMEM((surv, HEAD_DIM), F32),
            pltpu.VMEM((surv, 3 * HEAD_DIM), BF),
            pltpu.VMEM((heads, shards, 3, room, HEAD_DIM), BF),
            pltpu.VMEM((groups, width // groups, partial.shape[1]), BF),
            pltpu.VMEM((width // groups, partial.shape[1]), BF),
            pltpu.SemaphoreType.DMA((heads, shards)),
            pltpu.SemaphoreType.DMA((heads, shards)),
            pltpu.SemaphoreType.DMA((heads,)),
            pltpu.SemaphoreType.DMA((2, groups)),
            pltpu.SemaphoreType.DMA((2, groups)),
            pltpu.SemaphoreType.DMA((2,)),
        ],
        compiler_params=pltpu.CompilerParams(
            vmem_limit_bytes=VMEM_BYTES, collective_id=0, has_side_effects=True
        ),
        cost_estimate=pl.CostEstimate(
            flops=heads * surv * surv * 20000, bytes_accessed=heads * surv * surv * 4,
            transcendentals=0
        ),
        name="backward_heads",
    )(q, k, v, g, probs, pack, partial)


def place_kernel(place_ref, in_ref, sum_ref, out_ref, wide_ref):
    shards, heads, _, _, dim = in_ref.shape
    width = heads * dim

    @pl.when(pl.program_id(0) == 0)
    def _():
        wide_ref[...] = sum_ref[...].astype(F32)

    for shard in range(shards):
        held = jnp.concatenate([in_ref[shard, h, 0] for h in range(heads)], axis=1)
        out_ref[:, shard * width : (shard + 1) * width] = dot_nn(place_ref[...], held).astype(BF)


def place_rows(place, received, total):
    shards, heads, parts, room, dim = received.shape
    rows = place.shape[0]
    width = shards * heads * dim
    wide = pl.BlockSpec((total.shape[0] // 2, total.shape[1]), lambda p, s: (jnp.minimum(2 * p + s, 1), 0))
    return pl.pallas_call(
        place_kernel,
        grid=(parts, 2),
        in_specs=[
            pl.BlockSpec(place.shape, lambda p, s: (0, 0)),
            pl.BlockSpec((shards // 2, heads, 1, room, dim), lambda p, s: (s, 0, p, 0, 0)),
            wide,
        ],
        out_specs=[pl.BlockSpec((rows, width // 2), lambda p, s: (0, 2 * p + s)), wide],
        out_shape=[
            jax.ShapeDtypeStruct((rows, parts * width), BF),
            jax.ShapeDtypeStruct(total.shape, F32),
        ],
        compiler_params=pltpu.CompilerParams(vmem_limit_bytes=VMEM_BYTES),
        name="place_rows",
    )(place, received, total)


def body(places, grads, projector, queries, keys, values):
    shards = lax.axis_size("ctx")
    me = lax.axis_index("ctx")
    places = places[0]
    surv = places.shape[0]
    rows_here = grads.shape[1]
    room = rows_here * 3 // 4

    edges = jnp.arange(shards + 1, dtype=jnp.int32) * rows_here
    first = jnp.sum((places[None, :] < edges[:, None]).astype(jnp.int32), axis=1)
    slot = jnp.arange(room, dtype=jnp.int32)
    rank = first[:-1, None] + slot[None, :]
    rank = jnp.where(rank < first[1:, None], rank, -1).reshape(-1)
    pack = (rank[:, None] == jnp.arange(surv, dtype=jnp.int32)[None, :]).astype(BF)

    mine = lax.dynamic_slice_in_dim(rank, me * room, room)
    hit = mine[:, None] == jnp.arange(surv, dtype=jnp.int32)[None, :]
    local = jnp.sum(jnp.where(hit, places[None, :] - me * rows_here + 1, 0), axis=1) - 1
    row = jnp.arange(rows_here, dtype=jnp.int32)
    place = (row[:, None] == local[None, :]).astype(BF)
    compact = (local[:, None] == row[None, :]).astype(BF)

    q, k, v = queries[0], keys[0], values[0]
    probs, head_grads, partial = gather_forward(
        compact, grads[0], projector, pack, q, k, v, shards
    )
    received, total = backward_heads(
        q, k, v, head_grads, probs, pack, partial, shards, lax.axis_size("dp")
    )
    every_place, projector_derivative = place_rows(place, received, total)
    return (every_place[None], projector_derivative)


def solution(mesh):
    in_specs = (
        P("dp", None),
        P("dp", "ctx", None),
        P("ctx", None),
        P("dp", None, "ctx"),
        P("dp", None, "ctx"),
        P("dp", None, "ctx"),
    )
    out_specs = (P("dp", "ctx", None), P("ctx", None))
    return jax.shard_map(body, mesh=mesh, in_specs=in_specs, out_specs=out_specs, check_vma=False)
```

```python
import functools
import math

import jax
import jax.numpy as jnp
from jax import lax
from jax.experimental import pallas as pl
from jax.experimental.pallas import tpu as pltpu
from jax.sharding import PartitionSpec as P

HEAD_DIM = 128
BF = jnp.bfloat16
F32 = jnp.float32
VMEM_BYTES = 56 * 1024 * 1024


def dot_nn(a, b):
    return lax.dot_general(a, b, (((1,), (0,)), ((), ())), preferred_element_type=F32)


def dot_nt(a, b):
    return lax.dot_general(a, b, (((1,), (1,)), ((), ())), preferred_element_type=F32)


def dot_tn(a, b):
    return lax.dot_general(a, b, (((0,), (0,)), ((), ())), preferred_element_type=F32)


def query_blocks(surv):
    block = 256 if surv % 256 == 0 else surv
    return [(i * block, block) for i in range(surv // block)]


def gather_kernel(
    compact_ref, grads_ref, w_hbm, pack_hbm, q_hbm, k_hbm, v_hbm,
    probs_ref, head_grads_ref, partial_ref,
    w_ref, pack_ref, q_ref, k_ref, v_ref,
    blocks, stage, outputs, slot_outputs, picked_grads, total, send_sem, recv_sem, stage_sem, load_sem,
):
    shards, room, _ = blocks.shape
    surv, width = q_ref.shape
    heads = width // HEAD_DIM
    me, group = lax.axis_index("ctx"), lax.axis_index("dp")
    chips = shards // 2
    chip, core = me // 2, me % 2
    other = chip * 2 + (1 - core)
    after, before = lax.rem(me + 2, shards), lax.rem(me + shards - 2, shards)

    sources = (q_hbm, k_hbm, v_hbm, pack_hbm, w_hbm)
    targets = (q_ref, k_ref, v_ref, pack_ref, w_ref)
    loads = [
        pltpu.make_async_copy(source, target, load_sem.at[i])
        for i, (source, target) in enumerate(zip(sources, targets))
    ]
    for load in loads:
        load.start()

    barrier = pltpu.get_barrier_semaphore()
    for offset in range(1, shards):
        pl.semaphore_signal(
            barrier, inc=1, device_id=(group, lax.rem(me + offset, shards)),
            device_id_type=pl.DeviceIdType.MESH,
        )
    blocks[me] = dot_nn(compact_ref[...], grads_ref[...]).astype(BF)
    pl.semaphore_wait(barrier, shards - 1)

    def hop(slot, way, target):
        return pltpu.make_async_remote_copy(
            src_ref=blocks.at[slot],
            dst_ref=blocks.at[slot],
            send_sem=send_sem.at[way, slot],
            recv_sem=recv_sem.at[slot],
            device_id=(group, target),
            device_id_type=pl.DeviceIdType.MESH,
        )

    def up(slot):
        return hop(slot, 0, after)

    def down(slot):
        return hop(slot, 1, before)

    def across(slot):
        return hop(slot, 2, other)

    @pl.when(chip < chips - 1)
    def _():
        up(me).start()

    @pl.when(chip > 0)
    def _():
        down(me).start()

    across(me).start()
    for load in loads:
        load.wait()

    scale = 1.0 / math.sqrt(HEAD_DIM)

    def keep(head):
        return pltpu.make_async_copy(stage, probs_ref.at[head], stage_sem)

    def forward(head, carry):
        lanes = pl.ds(pl.multiple_of(head * HEAD_DIM, HEAD_DIM), HEAD_DIM)

        @pl.when(head > 0)
        def _():
            keep(head - 1).wait()

        for begin, size in query_blocks(surv):
            keys = begin + size
            scores = dot_nt(k_ref[0:keys, lanes], q_ref[begin:keys, lanes]) * scale
            key_at = lax.broadcasted_iota(jnp.int32, (keys, size), 0)
            query_at = lax.broadcasted_iota(jnp.int32, (keys, size), 1) + begin
            scores = jnp.where(key_at <= query_at, scores, -jnp.inf)
            exponent = jnp.exp(scores - jnp.max(scores, axis=0, keepdims=True))
            probs = exponent / jnp.sum(exponent, axis=0, keepdims=True)
            stage[0:keys, begin:keys] = probs
            outputs[begin:keys, lanes] = dot_tn(probs.astype(BF), v_ref[0:keys, lanes]).astype(BF)
        keep(head).start()
        return carry

    lax.fori_loop(0, heads, forward, 0)
    slot_outputs[...] = dot_nn(pack_ref[...], outputs[...]).astype(BF)
    keep(heads - 1).wait()

    def work(slot):
        rows = pl.ds(pl.multiple_of(slot * room, 16), room)
        slot_grads = dot_nt(blocks[slot], w_ref[...]).astype(BF)
        picked_grads[...] += dot_tn(pack_ref[rows, :], slot_grads)
        total[...] += dot_tn(slot_outputs[rows, :], blocks[slot])

    total[...] = jnp.zeros_like(total)
    picked_grads[...] = jnp.zeros_like(picked_grads)
    work(me)
    across(other).wait_recv()
    work(other)

    def step(distance, carry):
        lower, upper = chip - distance, chip + distance

        @pl.when(lower >= 0)
        def _():
            slot = lower * 2 + core
            up(slot).wait_recv()

            @pl.when(chip < chips - 1)
            def _():
                up(slot).start()

            across(slot).start()

        @pl.when(upper < chips)
        def _():
            slot = upper * 2 + core
            down(slot).wait_recv()

            @pl.when(chip > 0)
            def _():
                down(slot).start()

            across(slot).start()

        def each(which, inner):
            source = chip + (2 * (which % 2) - 1) * distance
            from_other = which // 2
            slot = source * 2 + core + from_other * (1 - 2 * core)

            @pl.when((source >= 0) & (source < chips))
            def _():
                @pl.when(from_other == 1)
                def _():
                    across(slot).wait_recv()

                work(slot)

            return inner

        lax.fori_loop(0, 4, each, 0)
        return carry

    lax.fori_loop(1, chips, step, 0)

    head_grads_ref[...] = picked_grads[...].astype(BF)
    partial_ref[...] = total[...].astype(BF)

    across(me).wait_send()

    @pl.when(chip < chips - 1)
    def _():
        up(me).wait_send()

    @pl.when(chip > 0)
    def _():
        down(me).wait_send()

    def finish(distance, carry):
        lower, upper = chip - distance, chip + distance

        @pl.when(lower >= 0)
        def _():
            across(lower * 2 + core).wait_send()

            @pl.when(chip < chips - 1)
            def _():
                up(lower * 2 + core).wait_send()

        @pl.when(upper < chips)
        def _():
            across(upper * 2 + core).wait_send()

            @pl.when(chip > 0)
            def _():
                down(upper * 2 + core).wait_send()

        return carry

    lax.fori_loop(1, chips, finish, 0)


def gather_forward(compact, grads, w, pack, q, k, v, shards):
    surv, width = q.shape
    heads = width // HEAD_DIM
    room = compact.shape[0]
    model = grads.shape[1]
    whole = pl.BlockSpec(memory_space=pltpu.VMEM)
    return pl.pallas_call(
        gather_kernel,
        in_specs=[whole] * 2 + [pl.BlockSpec(memory_space=pl.ANY)] * 5,
        out_specs=[pl.BlockSpec(memory_space=pl.ANY), whole, whole],
        out_shape=[
            jax.ShapeDtypeStruct((heads, surv, surv), F32),
            jax.ShapeDtypeStruct((surv, width), BF),
            jax.ShapeDtypeStruct((width, model), BF),
        ],
        scratch_shapes=[
            pltpu.VMEM(w.shape, BF),
            pltpu.VMEM(pack.shape, BF),
            pltpu.VMEM(q.shape, BF),
            pltpu.VMEM(q.shape, BF),
            pltpu.VMEM(q.shape, BF),
            pltpu.VMEM((shards, room, model), BF),
            pltpu.VMEM((surv, surv), F32),
            pltpu.VMEM((surv, width), BF),
            pltpu.VMEM((shards * room, width), BF),
            pltpu.VMEM((surv, width), F32),
            pltpu.VMEM((width, model), F32),
            pltpu.SemaphoreType.DMA((3, shards)),
            pltpu.SemaphoreType.DMA((shards,)),
            pltpu.SemaphoreType.DMA,
            pltpu.SemaphoreType.DMA((5,)),
        ],
        compiler_params=pltpu.CompilerParams(
            vmem_limit_bytes=VMEM_BYTES, collective_id=1, has_side_effects=True
        ),
        name="gather_forward",
    )(compact, grads, w, pack, q, k, v)


def backward_kernel(
    q_ref, k_ref, v_ref, g_ref, probs_ref, pack_ref, partial_ref,
    recv_ref, sum_ref,
    gk, gv, joined, outbox, inbox, summed,
    send_sem, recv_sem, own_sem, sum_send, sum_recv, sum_own,
):
    head = pl.program_id(0)
    heads, shards, _, room, _ = outbox.shape
    me, group = lax.axis_index("ctx"), lax.axis_index("dp")
    peers = [lax.rem(me + offset, shards) for offset in range(1, shards)]
    groups, piece, _ = inbox.shape
    others = [lax.rem(group + offset, groups) for offset in range(1, groups)]

    def piece_rows(owner):
        return pl.ds(pl.multiple_of(owner * piece, 16), piece)

    def scatter(owner, source):
        return pltpu.make_async_remote_copy(
            src_ref=partial_ref.at[piece_rows(owner)],
            dst_ref=inbox.at[source],
            send_sem=sum_send.at[0, owner],
            recv_sem=sum_recv.at[0, source],
            device_id=(owner, me),
            device_id_type=pl.DeviceIdType.MESH,
        )

    def spread(target, owner):
        return pltpu.make_async_remote_copy(
            src_ref=summed,
            dst_ref=sum_ref.at[piece_rows(owner)],
            send_sem=sum_send.at[1, target],
            recv_sem=sum_recv.at[1, owner],
            device_id=(target, me),
            device_id_type=pl.DeviceIdType.MESH,
        )

    scatter_own = pltpu.make_async_copy(
        partial_ref.at[piece_rows(group)], inbox.at[group], sum_own.at[0]
    )
    spread_own = pltpu.make_async_copy(summed, sum_ref.at[piece_rows(group)], sum_own.at[1])

    @pl.when(head == 0)
    def _():
        barrier = pltpu.get_barrier_semaphore()
        for peer in peers:
            pl.semaphore_signal(
                barrier, inc=1, device_id=(group, peer), device_id_type=pl.DeviceIdType.MESH
            )
        for target in others:
            pl.semaphore_signal(
                barrier, inc=1, device_id=(target, me), device_id_type=pl.DeviceIdType.MESH
            )
        pl.semaphore_wait(barrier, shards - 1 + groups - 1)
        for owner in others:
            scatter(owner, group).start()
        scatter_own.start()

    def outgoing(h, peer):
        return pltpu.make_async_remote_copy(
            src_ref=outbox.at[h, peer],
            dst_ref=recv_ref.at[me, h],
            send_sem=send_sem.at[h, peer],
            recv_sem=recv_sem.at[h, me],
            device_id=(group, peer),
            device_id_type=pl.DeviceIdType.MESH,
        )

    def incoming(h, peer):
        return pltpu.make_async_remote_copy(
            src_ref=outbox.at[h, peer],
            dst_ref=recv_ref.at[peer, h],
            send_sem=send_sem.at[h, peer],
            recv_sem=recv_sem.at[h, peer],
            device_id=(group, peer),
            device_id_type=pl.DeviceIdType.MESH,
        )

    def own(h):
        return pltpu.make_async_copy(outbox.at[h, me], recv_ref.at[me, h], own_sem.at[h])

    scale = 1.0 / math.sqrt(HEAD_DIM)
    surv = q_ref.shape[0]
    gk[...] = jnp.zeros_like(gk)
    gv[...] = jnp.zeros_like(gv)
    for begin, size in query_blocks(surv):
        keys = begin + size
        probs = probs_ref[0, 0:keys, begin:keys]
        grads = g_ref[begin:keys, :]
        dprobs = dot_nt(v_ref[0:keys, :], grads)
        center = jnp.sum(probs * dprobs, axis=0, keepdims=True)
        dscores = (probs * (dprobs - center) * scale).astype(BF)
        joined[begin:keys, 0:HEAD_DIM] = dot_tn(dscores, k_ref[0:keys, :]).astype(BF)
        gk[0:keys, :] += dot_nn(dscores, q_ref[begin:keys, :])
        gv[0:keys, :] += dot_nn(probs.astype(BF), grads)
    joined[:, HEAD_DIM : 2 * HEAD_DIM] = gk[...].astype(BF)
    joined[:, 2 * HEAD_DIM :] = gv[...].astype(BF)

    for peer in peers + [me]:
        slots = pl.ds(pl.multiple_of(peer * room, 16), room)
        packed = dot_nn(pack_ref[slots, :], joined[...]).astype(BF)
        for part in range(3):
            outbox[head, peer, part] = packed[:, part * HEAD_DIM : (part + 1) * HEAD_DIM]
        if peer is me:
            own(head).start()
        else:
            outgoing(head, peer).start()

    @pl.when(head == heads - 1)
    def _():
        scatter_own.wait()
        for source in others:
            scatter(source, source).wait_recv()
        run = inbox[0].astype(F32)
        for source in range(1, groups):
            run = run + inbox[source].astype(F32)
        summed[...] = run.astype(BF)
        for target in others:
            spread(target, group).start()
        spread_own.start()
        for h in range(heads):
            own(h).wait()
            for peer in peers:
                outgoing(h, peer).wait_send()
                incoming(h, peer).wait_recv()
        for target in others:
            scatter(target, group).wait_send()
            spread(target, group).wait_send()
            spread(target, target).wait_recv()
        spread_own.wait()


def backward_heads(q, k, v, g, probs, pack, partial, shards, groups):
    surv, width = q.shape
    heads = width // HEAD_DIM
    room = pack.shape[0] // shards
    rows = pl.BlockSpec((surv, HEAD_DIM), lambda h: (0, h))
    return pl.pallas_call(
        backward_kernel,
        grid=(heads,),
        in_specs=[rows] * 4
        + [
            pl.BlockSpec((1, surv, surv), lambda h: (h, 0, 0)),
            pl.BlockSpec(pack.shape, lambda h: (0, 0)),
            pl.BlockSpec(memory_space=pl.ANY),
        ],
        out_specs=[pl.BlockSpec(memory_space=pl.ANY)] * 2,
        out_shape=[
            jax.ShapeDtypeStruct((shards, heads, 3, room, HEAD_DIM), BF),
            jax.ShapeDtypeStruct(partial.shape, BF),
        ],
        scratch_shapes=[
            pltpu.VMEM((surv, HEAD_DIM), F32),
            pltpu.VMEM((surv, HEAD_DIM), F32),
            pltpu.VMEM((surv, 3 * HEAD_DIM), BF),
            pltpu.VMEM((heads, shards, 3, room, HEAD_DIM), BF),
            pltpu.VMEM((groups, width // groups, partial.shape[1]), BF),
            pltpu.VMEM((width // groups, partial.shape[1]), BF),
            pltpu.SemaphoreType.DMA((heads, shards)),
            pltpu.SemaphoreType.DMA((heads, shards)),
            pltpu.SemaphoreType.DMA((heads,)),
            pltpu.SemaphoreType.DMA((2, groups)),
            pltpu.SemaphoreType.DMA((2, groups)),
            pltpu.SemaphoreType.DMA((2,)),
        ],
        compiler_params=pltpu.CompilerParams(
            vmem_limit_bytes=VMEM_BYTES, collective_id=0, has_side_effects=True
        ),
        cost_estimate=pl.CostEstimate(
            flops=heads * surv * surv * 20000, bytes_accessed=heads * surv * surv * 4,
            transcendentals=0
        ),
        name="backward_heads",
    )(q, k, v, g, probs, pack, partial)


def place_kernel(place_ref, in_ref, sum_ref, out_ref, wide_ref):
    shards, heads, _, _, dim = in_ref.shape
    width = heads * dim

    @pl.when(pl.program_id(0) == 0)
    def _():
        wide_ref[...] = sum_ref[...].astype(F32)

    for shard in range(shards):
        held = jnp.concatenate([in_ref[shard, h, 0] for h in range(heads)], axis=1)
        out_ref[:, shard * width : (shard + 1) * width] = dot_nn(place_ref[...], held).astype(BF)


def place_rows(place, received, total):
    shards, heads, parts, room, dim = received.shape
    rows = place.shape[0]
    width = shards * heads * dim
    wide = pl.BlockSpec((total.shape[0] // 2, total.shape[1]), lambda p, s: (jnp.minimum(2 * p + s, 1), 0))
    return pl.pallas_call(
        place_kernel,
        grid=(parts, 2),
        in_specs=[
            pl.BlockSpec(place.shape, lambda p, s: (0, 0)),
            pl.BlockSpec((shards // 2, heads, 1, room, dim), lambda p, s: (s, 0, p, 0, 0)),
            wide,
        ],
        out_specs=[pl.BlockSpec((rows, width // 2), lambda p, s: (0, 2 * p + s)), wide],
        out_shape=[
            jax.ShapeDtypeStruct((rows, parts * width), BF),
            jax.ShapeDtypeStruct(total.shape, F32),
        ],
        compiler_params=pltpu.CompilerParams(vmem_limit_bytes=VMEM_BYTES),
        name="place_rows",
    )(place, received, total)


def body(places, grads, projector, queries, keys, values):
    shards = lax.axis_size("ctx")
    me = lax.axis_index("ctx")
    places = places[0]
    surv = places.shape[0]
    rows_here = grads.shape[1]
    room = rows_here * 3 // 4

    edges = jnp.arange(shards + 1, dtype=jnp.int32) * rows_here
    first = jnp.sum((places[None, :] < edges[:, None]).astype(jnp.int32), axis=1)
    slot = jnp.arange(room, dtype=jnp.int32)
    rank = first[:-1, None] + slot[None, :]
    rank = jnp.where(rank < first[1:, None], rank, -1).reshape(-1)
    pack = (rank[:, None] == jnp.arange(surv, dtype=jnp.int32)[None, :]).astype(BF)

    mine = lax.dynamic_slice_in_dim(rank, me * room, room)
    hit = mine[:, None] == jnp.arange(surv, dtype=jnp.int32)[None, :]
    local = jnp.sum(jnp.where(hit, places[None, :] - me * rows_here + 1, 0), axis=1) - 1
    row = jnp.arange(rows_here, dtype=jnp.int32)
    place = (row[:, None] == local[None, :]).astype(BF)
    compact = (local[:, None] == row[None, :]).astype(BF)

    q, k, v = queries[0], keys[0], values[0]
    probs, head_grads, partial = gather_forward(
        compact, grads[0], projector, pack, q, k, v, shards
    )
    received, total = backward_heads(
        q, k, v, head_grads, probs, pack, partial, shards, lax.axis_size("dp")
    )
    every_place, projector_derivative = place_rows(place, received, total)
    return (every_place[None], projector_derivative)


def solution(mesh):
    in_specs = (
        P("dp", None),
        P("dp", "ctx", None),
        P("ctx", None),
        P("dp", None, "ctx"),
        P("dp", None, "ctx"),
        P("dp", None, "ctx"),
    )
    out_specs = (P("dp", "ctx", None), P("ctx", None))
    return jax.shard_map(body, mesh=mesh, in_specs=in_specs, out_specs=out_specs, check_vma=False)
```
